32 devices in a mesh: diamond: 4 (over z), region: 8 (over y, x, core).
Axes of the slice: x: 2, y: 2, z: 4, core: 2. Of those that a mesh axis runs over, the one named last changes fastest.
Arguments:
- height: float32 [8, 256, 512], P(None, 'region', 'diamond'), may hold values from -6 to 6
- wind: float32 [2, 8, 256, 512], P(None, None, 'region', 'diamond'), may hold values from -6 to 6
- cell_area: float32 [256, 512], P('region', 'diamond'), may hold values from 0.5 to 2
- pentagon_flags: int32 [256, 512], P('region', 'diamond'), may hold values 0 or 1
- turn_codes: int32 [4], replicated, may hold values from 0 to 3
Outputs:
- new_height: float32 [8, 256, 512], P(None, 'region', 'diamond')
- new_wind: float32 [2, 8, 256, 512], P(None, None, 'region', 'diamond')
The draws below stay inside these ranges and needn't reach their ends.
All inputs are finite; a program needn't handle non-finite values. No bound on the sum of `pentagon_flags` on one device may be relied on, other than what follows from the above.
Results may differ from the reference program's by a relative error of at most 0.00002.
Values sent between devices are 32-bit elements; how exact they have to be, the bound alone decides.
A program may use at most 64 MiB of HBM per device.

```python
import math
import jax
import jax.numpy as jnp
from jax import lax

LEV = 8
CJ = 128
STEPS = 3
NDIAM = 4
NI = 256
NJ = 512
N_DIAMOND = 4


def draw_turn_codes(key, part):
    key = jax.random.fold_in(key, 7)
    key_codes = jax.random.fold_in(key, 1)
    key_places = jax.random.fold_in(key, 2)
    codes = jax.random.randint(key_codes, (NDIAM,), 0, 4, dtype=jnp.int32)
    places = jax.random.permutation(key_places, NDIAM)
    positions = jnp.arange(NDIAM, dtype=jnp.int32)
    codes = jnp.where(positions == places[0], 0, codes)
    codes = jnp.where(positions == places[1], 3, codes)
    return codes.astype(jnp.int32)


def plant(result, own_key, least, largest):
    index_at = [jax.random.randint(jax.random.fold_in(own_key, axis), (), 0, length) for axis, length in enumerate(result.shape)]
    longest = result.shape.index(max(result.shape))
    beside = index_at[:longest] + [(index_at[longest] + 1) % result.shape[longest]] + index_at[longest + 1:]
    return result.at[tuple(index_at)].set(least).at[tuple(beside)].set(largest)


def steps_of(key, extent, split, smallest, top_value):
    loudness = 1.0
    for dim, parts in split:
        draws = jax.random.uniform(jax.random.fold_in(jax.random.fold_in(key, 6), dim), (parts,), jnp.float32, smallest / len(split), top_value / len(split))
        loudness = loudness * jnp.repeat(jnp.exp(draws), extent[dim] // parts).reshape((-1,) + (1,) * (len(extent) - 1 - dim))
    return loudness


def bell_draw(key, dims, deviation, limit, split=(), kind=jnp.bfloat16):
    drawn = jax.random.normal(key, dims, jnp.float32) * deviation
    if len(split) > 0:
        drawn = steps_of(key, dims, split, -0.22, 0.18) * drawn
    return jnp.clip(drawn, min=-limit, max=limit).astype(kind)


def setup_inputs(seed: int = 0) -> dict:
    key_list = jax.random.split(jax.random.key(seed), 6)
    return {
        "height": bell_draw(key_list[0], (LEV, NI, NJ), 1.0, 6.0, ((1, 8), (2, 4)), jnp.float32),
        "wind": bell_draw(key_list[1], (2, LEV, NI, NJ), 1.0, 6.0, ((2, 8), (3, 4)), jnp.float32),
        "cell_area": jnp.clip(jnp.exp(math.log(2.0) - 1.3862944 * jax.random.uniform(key_list[2], (NI, NJ), jnp.float32) ** steps_of(key_list[2], (NI, NJ), ((0, 8), (1, 4)), -0.2, 0.2)), 0.5, 2.0),
        "pentagon_flags": plant((jax.random.randint(key_list[3], (NI, NJ), 0, 16) < 1).astype(jnp.int32), jax.random.fold_in(key_list[3], 1), 0, 1),
        "turn_codes": draw_turn_codes(jax.random.fold_in(key_list[5], 71), 0),
    }


time_step = 0.25
damping = 0.02


def rotate(east_part, north_part, code):
    cosine = jnp.where(code == 0, 1.0, jnp.where(code == 2, -1.0, 0.0))
    sine = jnp.where(code == 1, 1.0, jnp.where(code == 3, -1.0, 0.0))
    return east_part * cosine - north_part * sine, east_part * sine + north_part * cosine


def extend(field, width, turn_codes, vector):
    comps = field.shape[0]
    blocks = field.reshape(comps, NI, N_DIAMOND, CJ)
    left_part = jnp.roll(blocks, 1, axis=2)[..., CJ - width:]
    right_part = jnp.roll(blocks, -1, axis=2)[..., :width]
    if vector:
        left_code = jnp.mod(turn_codes - jnp.roll(turn_codes, 1), 4)[None, :, None]
        right_code = jnp.mod(turn_codes - jnp.roll(turn_codes, -1), 4)[None, :, None]
        left_part = jnp.stack(rotate(left_part[0], left_part[1], left_code))
        right_part = jnp.stack(rotate(right_part[0], right_part[1], right_code))
    wide = jnp.concatenate([left_part, blocks, right_part], axis=3)
    wide = jnp.concatenate([wide[:, NI - width:], wide, wide[:, :width]], axis=1)
    return jnp.transpose(wide, (0, 2, 1, 3))


def unblock(field):
    return jnp.transpose(field, (0, 2, 1, 3)).reshape(field.shape[0], NI, NJ)


def neighbours(field, penta):
    center = field[..., 1:-1, 1:-1]
    east = field[..., 1:-1, 2:]
    west = field[..., 1:-1, :-2]
    north = field[..., 2:, 1:-1]
    south = field[..., :-2, 1:-1]
    north_east = field[..., 2:, 2:]
    south_west = field[..., :-2, :-2]
    south_west = south_west + penta * (center - south_west)
    return center, east, west, north, south, north_east, south_west


def laplace(field, penta):
    center, east, west, north, south, north_east, south_west = neighbours(field, penta)
    return east + west + north + south + north_east + south_west - 6.0 * center


def gradient(field, penta):
    center, east, west, north, south, north_east, south_west = neighbours(field, penta)
    diagonal = (north_east - south_west) * 0.25
    return (east - west) * 0.5 + diagonal, (north - south) * 0.5 + diagonal


def divergence(height_ext, wind_ext, penta):
    depth = 1.0 + height_ext
    flux_east = neighbours(depth * wind_ext[0], penta)
    flux_north = neighbours(depth * wind_ext[1], penta)
    flux_diag = neighbours(depth * (wind_ext[0] + wind_ext[1]) * 0.5, penta)
    return ((flux_east[1] - flux_east[2]) + (flux_north[3] - flux_north[4]) + (flux_diag[5] - flux_diag[6])) * 0.5


def reference(height, wind, cell_area, pentagon_flags, turn_codes):
    penta = jnp.transpose(pentagon_flags.astype(jnp.float32).reshape(NI, N_DIAMOND, CJ), (1, 0, 2))

    def level(item):
        level_height, level_wind = item
        for number in range(STEPS):
            height_ext = extend(level_height[None], 1, turn_codes, False)[0]
            wind_ext = extend(level_wind, 1, turn_codes, True)
            first = unblock(laplace(wind_ext, penta))
            damp = laplace(extend(first, 1, turn_codes, True), penta)
            grad_east, grad_north = gradient(height_ext, penta)
            slope = jnp.stack([grad_east, grad_north])
            wind_next = level_wind - time_step * (unblock(slope) + damping * unblock(damp))
            wind_next_ext = extend(wind_next, 1, turn_codes, True)
            change = unblock(divergence(height_ext, wind_next_ext, penta)[None])[0]
            level_height = level_height - time_step * change / cell_area
            level_wind = wind_next
        return level_height, level_wind

    out_height, out_wind = lax.map(level, (height, jnp.moveaxis(wind, 1, 0)))
    return out_height, jnp.moveaxis(out_wind, 0, 1)
```

```python
import functools

import jax
import jax.numpy as jnp
from jax import lax
from jax.experimental import pallas as pl
from jax.experimental.pallas import tpu as pltpu
from jax.sharding import PartitionSpec as P

STEPS = 3
MESH = pl.DeviceIdType.MESH

time_step = 0.25
damping = 0.02

LEV, ROWS, LANES, PAD = 8, 32, 128, 8
EXT = ROWS + 2 * PAD
HALF = ROWS // 2
STRIP = HALF + 2 * PAD
FIELDS = 5


def shift_lanes(values, amount):
    amount = amount % LANES
    return values if amount == 0 else pltpu.roll(values, amount, values.ndim - 1)


def pieces(total, most):
    sizes = [n for n in range(1, 2 * most) if total % n == 0]
    size = max(n for n in sizes if n <= most)
    if size < most // 2:
        size = max(sizes)
    return total // size, size


def laplace(x, flag):
    count = x.shape[0] - 2
    east = shift_lanes(x[1:], -1)
    west = shift_lanes(x[:-1], 1)
    center = x[1:-1]
    south_west = jnp.where(flag, center, west[:count])
    return (
        ((east[:count] + west[1:]) + (x[2:] + x[:-2]))
        + (east[1:] + south_west)
        - 6.0 * center
    )


def step(state, lap, flux, radius, own_rows, most, basis):
    start = PAD - radius - 2
    count, size = pieces(own_rows + 2 * (radius + 2), most)

    def first(number, carry):
        at = start + number * size
        flag = state[4, pl.ds(at, size)] != 0.0
        for part in range(2):
            lap[part, pl.ds(at, size)] = laplace(state[1 + part, pl.ds(at - 1, size + 2)], flag)
        return carry

    lax.fori_loop(0, count, first, 0)

    start_wind = PAD - radius - 1
    count_wind, size_wind = pieces(own_rows + 2 * (radius + 1), most)

    def second(number, carry):
        at, size = start_wind + number * size_wind, size_wind
        flag = state[4, pl.ds(at, size)] != 0.0
        h = state[0, pl.ds(at - 1, size + 2)]
        center = h[1:-1]
        east = shift_lanes(h[1:], -1)
        west = shift_lanes(h[:-1], 1)
        south_west = jnp.where(flag, center, west[:size])
        diagonal = (east[1:] - south_west) * (0.25 * time_step)
        slope_east = (east[:size] - west[1:]) * (0.5 * time_step) + diagonal
        slope_north = (h[2:] - h[:-2]) * (0.5 * time_step) + diagonal
        if basis is not None:
            cosine, sine = basis
            slope_east, slope_north = (
                slope_east * cosine - slope_north * sine,
                slope_east * sine + slope_north * cosine,
            )
        depth = 1.0 + center
        for part, slope in ((0, slope_east), (1, slope_north)):
            damp = laplace(lap[part, pl.ds(at - 1, size + 2)], flag)
            wind = state[1 + part, pl.ds(at, size)] - (slope + (damping * time_step) * damp)
            state[1 + part, pl.ds(at, size)] = wind
            flux[part, pl.ds(at, size)] = depth * wind
        return carry

    lax.fori_loop(0, count_wind, second, 0)

    start_height = PAD - radius
    count_height, size_height = pieces(own_rows + 2 * radius, most)

    def third(number, carry):
        at, size = start_height + number * size_height, size_height
        flag = state[4, pl.ds(at, size)] != 0.0
        f1 = flux[0, pl.ds(at - 1, size + 2)]
        f2 = flux[1, pl.ds(at - 1, size + 2)]
        if basis is None:
            f3 = f1 + f2
            f3_east = shift_lanes(f3[2:], -1)
            f3_west = jnp.where(flag, f3[1:-1], shift_lanes(f3[:-2], 1))
            c1 = f1[1:-1]
            change = (
                (shift_lanes(c1, -1) - shift_lanes(c1, 1))
                + (f2[2:] - f2[:-2])
                + 0.5 * (f3_east - f3_west)
            )
        else:
            cosine, sine = basis

            def sides(f):
                east = shift_lanes(f[1:], -1)
                west = shift_lanes(f[:-1], 1)
                south_west = jnp.where(flag, f[1:-1], west[:size])
                return east[:size] - west[1:], f[2:] - f[:-2], 0.5 * (east[1:] - south_west)

            ew1, ns1, diag1 = sides(f1)
            ew2, ns2, diag2 = sides(f2)
            change = cosine * ((ew1 + ns2) + (diag1 + diag2)) + sine * (
                (ew2 - ns1) + (diag2 - diag1)
            )
        state[0, pl.ds(at, size)] = state[0, pl.ds(at, size)] - state[3, pl.ds(at, size)] * change
        return carry

    lax.fori_loop(0, count_height, third, 0)


def kernel(
    sizes, turns, height, wind, area, flags, out_height, out_wind,
    h_in, w_in, a_in, p_in, state, lap, flux, strip, strip_lap, strip_flux,
    edge, far, h_out, w_out, local_sem, row_send, row_recv, col_send, col_recv,
):
    diamonds, regions = sizes
    d, r = lax.axis_index("diamond"), lax.axis_index("region")
    left, right = lax.rem(d + diamonds - 1, diamonds), lax.rem(d + 1, diamonds)
    south, north = lax.rem(r + regions - 1, regions), lax.rem(r + 1, regions)

    own = [
        pltpu.make_async_copy(height, h_in.at[:, pl.ds(PAD, ROWS)], local_sem.at[0]),
        pltpu.make_async_copy(wind, w_in.at[:, :, pl.ds(PAD, ROWS)], local_sem.at[1]),
        pltpu.make_async_copy(area, a_in.at[pl.ds(PAD, ROWS)], local_sem.at[2]),
        pltpu.make_async_copy(flags, p_in.at[pl.ds(PAD, ROWS)], local_sem.at[3]),
    ]
    for copy in own:
        copy.start()
    barrier = pltpu.get_barrier_semaphore()
    around = [(x, y) for x in (left, d, right) for y in (south, r, north) if not (x is d and y is r)]
    for place in around:
        pl.semaphore_signal(barrier, inc=1, device_id=place, device_id_type=MESH)
    pl.semaphore_wait(barrier, 8)

    rows = []
    for way, (place, first, to) in enumerate(((south, 0, PAD + ROWS), (north, ROWS - PAD, 0))):
        src, dst = pl.ds(first, PAD), pl.ds(to, PAD)
        for number, (a, b) in enumerate((
            (height.at[:, src], h_in.at[:, dst]),
            (wind.at[:, :, src], w_in.at[:, :, dst]),
            (area.at[src], a_in.at[dst]),
            (flags.at[src], p_in.at[dst]),
        )):
            copy = pltpu.make_async_remote_copy(
                a, b, row_send.at[way, number], row_recv.at[way, number],
                device_id=(d, place), device_id_type=MESH,
            )
            copy.start()
            rows.append(copy)
    for copy in own:
        copy.wait()

    h_flat = h_in.reshape(LEV * EXT, LANES)
    w_flat = w_in.reshape(2 * LEV * EXT, LANES)

    def spread(i):
        state[0, i] = h_flat[pl.ds(i, LEV, stride=EXT), :]
        state[1, i] = w_flat[pl.ds(i, LEV, stride=EXT), :]
        state[2, i] = w_flat[pl.ds(LEV * EXT + i, LEV, stride=EXT), :]
        state[3, i] = jnp.broadcast_to((0.5 * time_step) / a_in[pl.ds(i, 1), :], (LEV, LANES))
        state[4, i] = jnp.broadcast_to(p_in[pl.ds(i, 1), :].astype(jnp.float32), (LEV, LANES))

    for i in range(PAD, PAD + ROWS):
        spread(i)

    lane = lax.broadcasted_iota(jnp.int32, (LEV, LANES), 1)

    def pack(field, carry):
        for half in range(2):
            first = jnp.zeros((LEV, LANES), jnp.float32)
            last = first
            for g in range(16):
                row = (g % 8) + 8 * half + (HALF if g >= 8 else 0)
                turned = shift_lanes(state[field, PAD + row], 8 * g)
                first = jnp.where((lane >= 8 * g) & (lane < 8 * g + 8), turned, first)
                before = (8 * g - 8) % LANES
                last = jnp.where((lane >= before) & (lane < before + 8), turned, last)
            edge[0, half, field] = first
            edge[1, half, field] = last
        return carry

    lax.fori_loop(0, FIELDS, pack, 0)
    columns = []
    for way, place in ((0, left), (1, right)):
        side = 1 - way
        for number, (a, b, region) in enumerate((
            (edge.at[way], far.at[side, pl.ds(0, 2)], r),
            (edge.at[way, 1], far.at[side, 2], north),
            (edge.at[way, 0], far.at[side, 3], south),
        )):
            copy = pltpu.make_async_remote_copy(
                a, b, col_send.at[way, number], col_recv.at[side, number],
                device_id=(place, region), device_id_type=MESH,
            )
            copy.start()
            columns.append(copy)

    for copy in rows:
        copy.wait_recv()
    for i in range(PAD):
        spread(i)
        spread(PAD + ROWS + i)

    in_half = lane % 64
    top = lane < 64
    left_halo, right_halo = in_half < 8, in_half >= 56
    left_group = in_half < 32

    def own_strip(number, carry):
        for field in range(FIELDS):
            low, high = state[field, number], state[field, number + HALF]
            strip[field, number] = jnp.where(
                left_group,
                jnp.where(top, shift_lanes(low, 8), shift_lanes(high, 72)),
                jnp.where(top, shift_lanes(low, 56), shift_lanes(high, 120)),
            )
        return carry

    lax.fori_loop(0, STRIP, own_strip, 0)

    for number in range(STEPS):
        step(state, lap, flux, 2 * (STEPS - 1 - number), ROWS, 12, None)

    def turn(other):
        code = turns[d] - turns[other]
        code = jnp.where(code < 0, code + 4, code)
        return (
            jnp.where(code == 0, 1.0, jnp.where(code == 2, -1.0, 0.0)),
            jnp.where(code == 1, 1.0, jnp.where(code == 3, -1.0, 0.0)),
        )

    left_turn, right_turn = turn(left), turn(right)
    cosine = jnp.where(left_halo, left_turn[0], jnp.where(right_halo, right_turn[0], 1.0))
    sine = jnp.where(left_halo, left_turn[1], jnp.where(right_halo, right_turn[1], 0.0))

    for copy in columns:
        copy.wait_recv()

    first_rows = top
    first_rows_before = (lane < 56) | (lane >= 120)

    def blocks(side, field, mask):
        q1, q2, from_south, from_north = [far[side, n, field] for n in range(4)]
        return (
            shift_lanes(jnp.where(mask, q2, from_south), 64),
            q1,
            q2,
            shift_lanes(jnp.where(mask, from_north, q1), 64),
        )

    for block in range(STRIP // 8):
        near = []
        for field in range(FIELDS):
            near.append((
                blocks(0, field, first_rows_before)[block],
                blocks(1, field, first_rows)[block],
            ))
        for g in range(8):
            at = 8 * block + g
            values = []
            for field in range(FIELDS):
                from_left, from_right = near[field]
                values.append(jnp.where(
                    left_halo,
                    shift_lanes(from_left, 8 - 8 * g),
                    jnp.where(right_halo, shift_lanes(from_right, 56 - 8 * g), strip[field, at]),
                ))
            strip[0, at] = values[0]
            strip[1, at] = values[1] * cosine - values[2] * sine
            strip[2, at] = values[1] * sine + values[2] * cosine
            strip[3, at] = values[3]
            strip[4, at] = values[4]

    for number in range(STEPS):
        step(strip, strip_lap, strip_flux, 2 * (STEPS - 1 - number), HALF, 12, (cosine, sine))

    h_rows = h_out.reshape(LEV * ROWS, LANES)
    w_rows = w_out.reshape(2 * LEV * ROWS, LANES)
    for i in range(HALF):
        for field in range(3):
            both = strip[field, PAD + i]
            for row, to_left, to_right in ((i, -8, 72), (i + HALF, 56, 8)):
                value = jnp.where(
                    lane < 8,
                    shift_lanes(both, to_left),
                    jnp.where(lane >= 120, shift_lanes(both, to_right), state[field, PAD + row]),
                )
                if field == 0:
                    h_rows[pl.ds(row, LEV, stride=ROWS), :] = value
                else:
                    w_rows[pl.ds((field - 1) * LEV * ROWS + row, LEV, stride=ROWS), :] = value
    done = [
        pltpu.make_async_copy(h_out, out_height, local_sem.at[0]),
        pltpu.make_async_copy(w_out, out_wind, local_sem.at[1]),
    ]
    for copy in done:
        copy.start()
    for copy in rows + columns:
        copy.wait_send()
    for copy in done:
        copy.wait()


def body(sizes, height, wind, cell_area, pentagon_flags, turn_codes):
    any_space = pl.BlockSpec(memory_space=pl.ANY)
    f32 = jnp.float32
    return tuple(pl.pallas_call(
        functools.partial(kernel, sizes),
        out_shape=(
            jax.ShapeDtypeStruct(height.shape, f32),
            jax.ShapeDtypeStruct(wind.shape, f32),
        ),
        in_specs=[pl.BlockSpec(memory_space=pltpu.SMEM)] + [any_space] * 4,
        out_specs=(any_space, any_space),
        scratch_shapes=[
            pltpu.VMEM((LEV, EXT, LANES), f32),
            pltpu.VMEM((2, LEV, EXT, LANES), f32),
            pltpu.VMEM((EXT, LANES), f32),
            pltpu.VMEM((EXT, LANES), jnp.int32),
            pltpu.VMEM((FIELDS, EXT, LEV, LANES), f32),
            pltpu.VMEM((2, EXT, LEV, LANES), f32),
            pltpu.VMEM((2, EXT, LEV, LANES), f32),
            pltpu.VMEM((FIELDS, STRIP, LEV, LANES), f32),
            pltpu.VMEM((2, STRIP, LEV, LANES), f32),
            pltpu.VMEM((2, STRIP, LEV, LANES), f32),
            pltpu.VMEM((2, 2, FIELDS, LEV, LANES), f32),
            pltpu.VMEM((2, 4, FIELDS, LEV, LANES), f32),
            pltpu.VMEM((LEV, ROWS, LANES), f32),
            pltpu.VMEM((2, LEV, ROWS, LANES), f32),
            pltpu.SemaphoreType.DMA((4,)),
            pltpu.SemaphoreType.DMA((2, 4)),
            pltpu.SemaphoreType.DMA((2, 4)),
            pltpu.SemaphoreType.DMA((2, 3)),
            pltpu.SemaphoreType.DMA((2, 3)),
        ],
        compiler_params=pltpu.CompilerParams(
            collective_id=0, has_side_effects=True, vmem_limit_bytes=32 * 1024 * 1024
        ),
    )(turn_codes, height, wind, cell_area, pentagon_flags))


def solution(mesh):
    placed = (
        P(None, "region", "diamond"),
        P(None, None, "region", "diamond"),
        P("region", "diamond"),
        P("region", "diamond"),
        P(),
    )
    sizes = (mesh.shape["diamond"], mesh.shape["region"])
    return jax.shard_map(
        functools.partial(body, sizes),
        mesh=mesh,
        in_specs=placed,
        out_specs=(P(None, "region", "diamond"), P(None, None, "region", "diamond")),
        check_vma=False,
    )
```

```python
import functools

import jax
import jax.numpy as jnp
from jax import lax
from jax.experimental import pallas as pl
from jax.experimental.pallas import tpu as pltpu
from jax.sharding import PartitionSpec as P

STEPS = 3
MESH = pl.DeviceIdType.MESH

time_step = 0.25
damping = 0.02

LEV, ROWS, LANES, PAD = 8, 32, 128, 8
EXT = ROWS + 2 * PAD
HALF = ROWS // 2
STRIP = HALF + 2 * PAD
FIELDS = 5


def shift_lanes(values, amount):
    amount = amount % LANES
    return values if amount == 0 else pltpu.roll(values, amount, values.ndim - 1)


def pieces(total, most):
    sizes = [n for n in range(1, 2 * most) if total % n == 0]
    size = max(n for n in sizes if n <= most)
    if size < most // 2:
        size = max(sizes)
    return total // size, size


def laplace(x, flag):
    count = x.shape[0] - 2
    east = shift_lanes(x[1:], -1)
    west = shift_lanes(x[:-1], 1)
    center = x[1:-1]
    south_west = jnp.where(flag, center, west[:count])
    return (
        ((east[:count] + west[1:]) + (x[2:] + x[:-2]))
        + (east[1:] + south_west)
        - 6.0 * center
    )


def each(count, run):
    def once(number, carry):
        run(number)
        return carry

    lax.fori_loop(0, count, once, 0, unroll=True)


def first_laplace(buffers, at, size, basis):
    state, lap, flux = buffers
    flag = state[4, pl.ds(at, size)] != 0.0
    for part in range(2):
        lap[part, pl.ds(at, size)] = laplace(state[1 + part, pl.ds(at - 1, size + 2)], flag)


def next_wind(buffers, at, size, basis):
    state, lap, flux = buffers
    flag = state[4, pl.ds(at, size)] != 0.0
    h = state[0, pl.ds(at - 1, size + 2)]
    center = h[1:-1]
    east = shift_lanes(h[1:], -1)
    west = shift_lanes(h[:-1], 1)
    south_west = jnp.where(flag, center, west[:size])
    diagonal = (east[1:] - south_west) * (0.25 * time_step)
    slope_east = (east[:size] - west[1:]) * (0.5 * time_step) + diagonal
    slope_north = (h[2:] - h[:-2]) * (0.5 * time_step) + diagonal
    if basis is not None:
        cosine, sine = basis
        slope_east, slope_north = (
            slope_east * cosine - slope_north * sine,
            slope_east * sine + slope_north * cosine,
        )
    depth = 1.0 + center
    for part, slope in ((0, slope_east), (1, slope_north)):
        damp = laplace(lap[part, pl.ds(at - 1, size + 2)], flag)
        wind = state[1 + part, pl.ds(at, size)] - (slope + (damping * time_step) * damp)
        state[1 + part, pl.ds(at, size)] = wind
        flux[part, pl.ds(at, size)] = depth * wind


def next_height(buffers, at, size, basis):
    state, lap, flux = buffers
    flag = state[4, pl.ds(at, size)] != 0.0
    f1 = flux[0, pl.ds(at - 1, size + 2)]
    f2 = flux[1, pl.ds(at - 1, size + 2)]
    if basis is None:
        f3 = f1 + f2
        f3_east = shift_lanes(f3[2:], -1)
        f3_west = jnp.where(flag, f3[1:-1], shift_lanes(f3[:-2], 1))
        c1 = f1[1:-1]
        change = (
            (shift_lanes(c1, -1) - shift_lanes(c1, 1))
            + (f2[2:] - f2[:-2])
            + 0.5 * (f3_east - f3_west)
        )
    else:
        cosine, sine = basis

        def sides(f):
            east = shift_lanes(f[1:], -1)
            west = shift_lanes(f[:-1], 1)
            south_west = jnp.where(flag, f[1:-1], west[:size])
            return east[:size] - west[1:], f[2:] - f[:-2], 0.5 * (east[1:] - south_west)

        ew1, ns1, diag1 = sides(f1)
        ew2, ns2, diag2 = sides(f2)
        change = cosine * ((ew1 + ns2) + (diag1 + diag2)) + sine * (
            (ew2 - ns1) + (diag2 - diag1)
        )
    state[0, pl.ds(at, size)] = state[0, pl.ds(at, size)] - state[3, pl.ds(at, size)] * change


STAGES = (first_laplace, next_wind, next_height)


def inner(buffers, own_rows, most, basis):
    for stage in range(3 * STEPS):
        number, kind = divmod(stage, 3)
        skip = 2 * number + 1 + kind
        count, size = pieces(own_rows - 2 * skip, most)
        each(count, lambda n: STAGES[kind](buffers, PAD + skip + n * size, size, basis))


def outer(buffers, own_rows, basis):
    for stage in range(3 * STEPS):
        number, kind = divmod(stage, 3)
        skip = 2 * number + 1 + kind
        beyond = 2 * (STEPS - number) - kind
        far_start = PAD + own_rows - skip
        near_start = PAD - beyond
        each(2, lambda n: STAGES[kind](
            buffers, near_start + n * (far_start - near_start), skip + beyond, basis))


def kernel(
    sizes, turn_codes, height, wind, area, flags, h_out, w_out, turns,
    h_in, w_in, a_in, p_in, state, lap, flux, strip, strip_lap, strip_flux,
    edge, far, local_sem, row_send, row_recv, col_send, col_recv,
):
    diamonds, regions = sizes
    d, r = lax.axis_index("diamond"), lax.axis_index("region")
    left, right = lax.rem(d + diamonds - 1, diamonds), lax.rem(d + 1, diamonds)
    south, north = lax.rem(r + regions - 1, regions), lax.rem(r + 1, regions)

    own = [
        pltpu.make_async_copy(height, h_in.at[:, pl.ds(PAD, ROWS)], local_sem.at[0]),
        pltpu.make_async_copy(wind, w_in.at[:, :, pl.ds(PAD, ROWS)], local_sem.at[1]),
        pltpu.make_async_copy(area, a_in.at[pl.ds(PAD, ROWS)], local_sem.at[2]),
        pltpu.make_async_copy(flags, p_in.at[pl.ds(PAD, ROWS)], local_sem.at[3]),
        pltpu.make_async_copy(turn_codes, turns, local_sem.at[4]),
    ]
    for copy in own:
        copy.start()
    barrier = pltpu.get_barrier_semaphore()
    around = [(x, y) for x in (left, d, right) for y in (south, r, north) if not (x is d and y is r)]
    for place in around:
        pl.semaphore_signal(barrier, inc=1, device_id=place, device_id_type=MESH)
    pl.semaphore_wait(barrier, 8)

    rows = []
    for way, (place, first, to) in enumerate(((south, 0, PAD + ROWS), (north, ROWS - PAD, 0))):
        src, dst = pl.ds(first, PAD), pl.ds(to, PAD)
        for number, (a, b) in enumerate((
            (height.at[:, src], h_in.at[:, dst]),
            (wind.at[:, :, src], w_in.at[:, :, dst]),
            (area.at[src], a_in.at[dst]),
            (flags.at[src], p_in.at[dst]),
        )):
            copy = pltpu.make_async_remote_copy(
                a, b, row_send.at[way, number], row_recv.at[way, number],
                device_id=(d, place), device_id_type=MESH,
            )
            copy.start()
            rows.append(copy)
    for copy in own:
        copy.wait()

    h_flat = h_in.reshape(LEV * EXT, LANES)
    w_flat = w_in.reshape(2 * LEV * EXT, LANES)

    def given(field, i):
        if field == 0:
            return h_flat[pl.ds(i, LEV, stride=EXT), :]
        if field < 3:
            return w_flat[pl.ds((field - 1) * LEV * EXT + i, LEV, stride=EXT), :]
        return state[field, i]

    def spread(i):
        for field in range(3):
            state[field, i] = given(field, i)
        state[3, i] = jnp.broadcast_to((0.5 * time_step) / a_in[pl.ds(i, 1), :], (LEV, LANES))
        state[4, i] = jnp.broadcast_to(p_in[pl.ds(i, 1), :].astype(jnp.float32), (LEV, LANES))

    for i in range(PAD, PAD + ROWS):
        spread(i)

    lane = lax.broadcasted_iota(jnp.int32, (LEV, LANES), 1)

    def pack(field, carry):
        for half in range(2):
            first = jnp.zeros((LEV, LANES), jnp.float32)
            last = first
            for g in range(16):
                row = (g % 8) + 8 * half + (HALF if g >= 8 else 0)
                turned = shift_lanes(state[field, PAD + row], 8 * g)
                first = jnp.where((lane >= 8 * g) & (lane < 8 * g + 8), turned, first)
                before = (8 * g - 8) % LANES
                last = jnp.where((lane >= before) & (lane < before + 8), turned, last)
            edge[0, half, field] = first
            edge[1, half, field] = last
        return carry

    lax.fori_loop(0, FIELDS, pack, 0)
    columns = []
    for way, place in ((0, left), (1, right)):
        side = 1 - way
        for number, (a, b, region) in enumerate((
            (edge.at[way], far.at[side, pl.ds(0, 2)], r),
            (edge.at[way, 1], far.at[side, 2], north),
            (edge.at[way, 0], far.at[side, 3], south),
        )):
            copy = pltpu.make_async_remote_copy(
                a, b, col_send.at[way, number], col_recv.at[side, number],
                device_id=(place, region), device_id_type=MESH,
            )
            copy.start()
            columns.append((number, copy))

    main = (state, lap, flux)
    inner(main, ROWS, 10, None)

    in_half = lane % 64
    top = lane < 64
    left_halo, right_halo = in_half < 8, in_half >= 56
    left_group = in_half < 32
    top_before = (lane < 56) | (lane >= 120)

    def turn(other):
        code = turns[d] - turns[other]
        code = jnp.where(code < 0, code + 4, code)
        return (
            jnp.where(code == 0, 1.0, jnp.where(code == 2, -1.0, 0.0)),
            jnp.where(code == 1, 1.0, jnp.where(code == 3, -1.0, 0.0)),
        )

    left_turn, right_turn = turn(left), turn(right)
    cosine = jnp.where(left_halo, left_turn[0], jnp.where(right_halo, right_turn[0], 1.0))
    sine = jnp.where(left_halo, left_turn[1], jnp.where(right_halo, right_turn[1], 0.0))
    basis = (cosine, sine)

    def received(block, side, field, mask):
        if block == 0:
            both = jnp.where(mask, far[side, 1, field], far[side, 2, field])
            return shift_lanes(both, 64)
        if block == 3:
            both = jnp.where(mask, far[side, 3, field], far[side, 0, field])
            return shift_lanes(both, 64)
        return far[side, block - 1, field]

    def build(block):
        def one(field):
            from_left = received(block, 0, field, top_before)
            from_right = received(block, 1, field, top)
            for g in range(8):
                at = 8 * block + g
                low, high = given(field, at), given(field, at + HALF)
                mine = jnp.where(
                    left_group,
                    jnp.where(top, shift_lanes(low, 8), shift_lanes(high, 72)),
                    jnp.where(top, shift_lanes(low, 56), shift_lanes(high, 120)),
                )
                strip[field, at] = jnp.where(
                    left_halo,
                    shift_lanes(from_left, 8 - 8 * g),
                    jnp.where(right_halo, shift_lanes(from_right, 56 - 8 * g), mine),
                )

        for field in range(FIELDS):
            one(field)
        where = pl.ds(8 * block, 8)
        east, north = strip[1, where], strip[2, where]
        strip[1, where] = east * cosine - north * sine
        strip[2, where] = east * sine + north * cosine

    edges = (strip, strip_lap, strip_flux)
    for copy in columns:
        if copy[0] == 0:
            copy[1].wait_recv()
    build(1)
    build(2)
    inner(edges, HALF, 10, basis)

    for copy in rows:
        copy.wait_recv()
    for i in range(PAD):
        spread(i)
        spread(PAD + ROWS + i)
    for copy in columns:
        if copy[0] != 0:
            copy[1].wait_recv()
    build(0)
    build(3)
    outer(main, ROWS, None)
    outer(edges, HALF, basis)

    h_rows = h_out.reshape(LEV * ROWS, LANES)
    w_rows = w_out.reshape(2 * LEV * ROWS, LANES)
    for i in range(HALF):
        for field in range(3):
            both = strip[field, PAD + i]
            for row, to_left, to_right in ((i, -8, 72), (i + HALF, 56, 8)):
                value = jnp.where(
                    lane < 8,
                    shift_lanes(both, to_left),
                    jnp.where(lane >= 120, shift_lanes(both, to_right), state[field, PAD + row]),
                )
                if field == 0:
                    h_rows[pl.ds(row, LEV, stride=ROWS), :] = value
                else:
                    w_rows[pl.ds((field - 1) * LEV * ROWS + row, LEV, stride=ROWS), :] = value
    for copy in rows + [copy for _, copy in columns]:
        copy.wait_send()


def body(sizes, height, wind, cell_area, pentagon_flags, turn_codes):
    hbm = pl.BlockSpec(memory_space=pltpu.HBM)
    vmem = pl.BlockSpec(memory_space=pltpu.VMEM)
    f32 = jnp.float32
    return tuple(pl.pallas_call(
        functools.partial(kernel, sizes),
        out_shape=(
            jax.ShapeDtypeStruct(height.shape, f32),
            jax.ShapeDtypeStruct(wind.shape, f32),
        ),
        in_specs=[hbm] * 5,
        out_specs=(vmem, vmem),
        scratch_shapes=[
            pltpu.SMEM(turn_codes.shape, jnp.int32),
            pltpu.VMEM((LEV, EXT, LANES), f32),
            pltpu.VMEM((2, LEV, EXT, LANES), f32),
            pltpu.VMEM((EXT, LANES), f32),
            pltpu.VMEM((EXT, LANES), jnp.int32),
            pltpu.VMEM((FIELDS, EXT, LEV, LANES), f32),
            pltpu.VMEM((2, EXT, LEV, LANES), f32),
            pltpu.VMEM((2, EXT, LEV, LANES), f32),
            pltpu.VMEM((FIELDS, STRIP, LEV, LANES), f32),
            pltpu.VMEM((2, STRIP, LEV, LANES), f32),
            pltpu.VMEM((2, STRIP, LEV, LANES), f32),
            pltpu.VMEM((2, 2, FIELDS, LEV, LANES), f32),
            pltpu.VMEM((2, 4, FIELDS, LEV, LANES), f32),
            pltpu.SemaphoreType.DMA((5,)),
            pltpu.SemaphoreType.DMA((2, 4)),
            pltpu.SemaphoreType.DMA((2, 4)),
            pltpu.SemaphoreType.DMA((2, 3)),
            pltpu.SemaphoreType.DMA((2, 3)),
        ],
        compiler_params=pltpu.CompilerParams(
            collective_id=0, has_side_effects=True, vmem_limit_bytes=32 * 1024 * 1024
        ),
    )(*[
        pltpu.with_memory_space_constraint(x, pltpu.HBM)
        for x in (turn_codes, height, wind, cell_area, pentagon_flags)
    ]))


def solution(mesh):
    placed = (
        P(None, "region", "diamond"),
        P(None, None, "region", "diamond"),
        P("region", "diamond"),
        P("region", "diamond"),
        P(),
    )
    sizes = (mesh.shape["diamond"], mesh.shape["region"])
    return jax.shard_map(
        functools.partial(body, sizes),
        mesh=mesh,
        in_specs=placed,
        out_specs=(P(None, "region", "diamond"), P(None, None, "region", "diamond")),
        check_vma=False,
    )
```

```python
import functools

import jax
import jax.numpy as jnp
from jax import lax
from jax.experimental import pallas as pl
from jax.experimental.pallas import tpu as pltpu
from jax.sharding import PartitionSpec as P

STEPS = 3
MESH = pl.DeviceIdType.MESH

time_step = 0.25
damping = 0.02

LEV, ROWS, LANES, PAD = 8, 32, 128, 8
EXT = ROWS + 2 * PAD
HALF = ROWS // 2
STRIP = HALF + 2 * PAD
FIELDS = 5
SENT = 4


def shift_lanes(values, amount):
    amount = amount % LANES
    return values if amount == 0 else pltpu.roll(values, amount, values.ndim - 1)


def pieces(total, most):
    sizes = [n for n in range(1, 2 * most) if total % n == 0]
    size = max(n for n in sizes if n <= most)
    if size < most // 2:
        size = max(sizes)
    return total // size, size


def laplace(x, flag):
    count = x.shape[0] - 2
    east = shift_lanes(x[1:], -1)
    west = shift_lanes(x[:-1], 1)
    center = x[1:-1]
    south_west = jnp.where(flag, center, west[:count])
    return (
        ((east[:count] + west[1:]) + (x[2:] + x[:-2]))
        + (east[1:] + south_west)
        - 6.0 * center
    )


def each(count, run):
    def once(number, carry):
        run(number)
        return carry

    lax.fori_loop(0, count, once, 0, unroll=True)


def first_laplace(buffers, at, size, basis):
    state, lap, flux = buffers
    flag = state[4, pl.ds(at, size)] != 0.0
    for part in range(2):
        lap[part, pl.ds(at, size)] = laplace(state[1 + part, pl.ds(at - 1, size + 2)], flag)


def next_wind(buffers, at, size, basis):
    state, lap, flux = buffers
    flag = state[4, pl.ds(at, size)] != 0.0
    h = state[0, pl.ds(at - 1, size + 2)]
    center = h[1:-1]
    east = shift_lanes(h[1:], -1)
    west = shift_lanes(h[:-1], 1)
    south_west = jnp.where(flag, center, west[:size])
    diagonal = (east[1:] - south_west) * (0.25 * time_step)
    slope_east = (east[:size] - west[1:]) * (0.5 * time_step) + diagonal
    slope_north = (h[2:] - h[:-2]) * (0.5 * time_step) + diagonal
    if basis is not None:
        cosine, sine = basis
        slope_east, slope_north = (
            slope_east * cosine - slope_north * sine,
            slope_east * sine + slope_north * cosine,
        )
    depth = 1.0 + center
    for part, slope in ((0, slope_east), (1, slope_north)):
        damp = laplace(lap[part, pl.ds(at - 1, size + 2)], flag)
        wind = state[1 + part, pl.ds(at, size)] - (slope + (damping * time_step) * damp)
        state[1 + part, pl.ds(at, size)] = wind
        flux[part, pl.ds(at, size)] = depth * wind


def next_height(buffers, at, size, basis):
    state, lap, flux = buffers
    flag = state[4, pl.ds(at, size)] != 0.0
    f1 = flux[0, pl.ds(at - 1, size + 2)]
    f2 = flux[1, pl.ds(at - 1, size + 2)]
    if basis is None:
        f3 = f1 + f2
        f3_east = shift_lanes(f3[2:], -1)
        f3_west = jnp.where(flag, f3[1:-1], shift_lanes(f3[:-2], 1))
        c1 = f1[1:-1]
        change = (
            (shift_lanes(c1, -1) - shift_lanes(c1, 1))
            + (f2[2:] - f2[:-2])
            + 0.5 * (f3_east - f3_west)
        )
    else:
        cosine, sine = basis

        def sides(f):
            east = shift_lanes(f[1:], -1)
            west = shift_lanes(f[:-1], 1)
            south_west = jnp.where(flag, f[1:-1], west[:size])
            return east[:size] - west[1:], f[2:] - f[:-2], 0.5 * (east[1:] - south_west)

        ew1, ns1, diag1 = sides(f1)
        ew2, ns2, diag2 = sides(f2)
        change = cosine * ((ew1 + ns2) + (diag1 + diag2)) + sine * (
            (ew2 - ns1) + (diag2 - diag1)
        )
    state[0, pl.ds(at, size)] = state[0, pl.ds(at, size)] - state[3, pl.ds(at, size)] * change


STAGES = (first_laplace, next_wind, next_height)


def inner(buffers, own_rows, most, basis):
    for stage in range(3 * STEPS):
        number, kind = divmod(stage, 3)
        skip = 2 * number + 1 + kind
        count, size = pieces(own_rows - 2 * skip, most)
        each(count, lambda n: STAGES[kind](buffers, PAD + skip + n * size, size, basis))


def outer(parts):
    for stage in range(3 * STEPS):
        number, kind = divmod(stage, 3)
        skip = 2 * number + 1 + kind
        beyond = 2 * (STEPS - number) - kind
        for buffers, own_rows, basis in parts:
            for at in (PAD - beyond, PAD + own_rows - skip):
                STAGES[kind](buffers, at, skip + beyond, basis)


def kernel(
    sizes, turn_codes, height, wind, area, flags, h_out, w_out, turns,
    h_in, w_in, a_in, p_in, state, lap, flux, strip, strip_lap, strip_flux,
    edge, corner, far, far_corner, local_sem, row_send, row_recv, col_send, col_recv,
):
    diamonds, regions = sizes
    d, r = lax.axis_index("diamond"), lax.axis_index("region")
    left, right = lax.rem(d + diamonds - 1, diamonds), lax.rem(d + 1, diamonds)
    south, north = lax.rem(r + regions - 1, regions), lax.rem(r + 1, regions)

    own = [
        pltpu.make_async_copy(height, h_in.at[:, pl.ds(PAD, ROWS)], local_sem.at[0]),
        pltpu.make_async_copy(wind, w_in.at[:, :, pl.ds(PAD, ROWS)], local_sem.at[1]),
        pltpu.make_async_copy(area, a_in.at[pl.ds(PAD, ROWS)], local_sem.at[2]),
        pltpu.make_async_copy(flags, p_in.at[pl.ds(PAD, ROWS)], local_sem.at[3]),
        pltpu.make_async_copy(turn_codes, turns, local_sem.at[4]),
    ]
    for copy in own:
        copy.start()
    barrier = pltpu.get_barrier_semaphore()
    around = [(x, y) for x in (left, d, right) for y in (south, r, north) if not (x is d and y is r)]
    for place in around:
        pl.semaphore_signal(barrier, inc=1, device_id=place, device_id_type=MESH)
    pl.semaphore_wait(barrier, 8)

    rows = []
    for way, (place, first, to) in enumerate(((south, 0, PAD + ROWS), (north, ROWS - PAD, 0))):
        src, dst = pl.ds(first, PAD), pl.ds(to, PAD)
        for number, (a, b) in enumerate((
            (height.at[:, src], h_in.at[:, dst]),
            (wind.at[:, :, src], w_in.at[:, :, dst]),
            (area.at[src], a_in.at[dst]),
            (flags.at[src], p_in.at[dst]),
        )):
            copy = pltpu.make_async_remote_copy(
                a, b, row_send.at[way, number], row_recv.at[way, number],
                device_id=(d, place), device_id_type=MESH,
            )
            copy.start()
            rows.append(copy)
    for copy in own:
        copy.wait()

    h_flat = h_in.reshape(LEV * EXT, LANES)
    w_flat = w_in.reshape(2 * LEV * EXT, LANES)

    def given(field, i):
        if field == 0:
            return h_flat[pl.ds(i, LEV, stride=EXT), :]
        if field < 3:
            return w_flat[pl.ds((field - 1) * LEV * EXT + i, LEV, stride=EXT), :]
        return state[field, i]

    def spread(i):
        for field in range(3):
            state[field, i] = given(field, i)
        state[3, i] = jnp.broadcast_to((0.5 * time_step) / a_in[pl.ds(i, 1), :], (LEV, LANES))
        state[4, i] = jnp.broadcast_to(p_in[pl.ds(i, 1), :].astype(jnp.float32), (LEV, LANES))

    for i in range(PAD, PAD + ROWS):
        spread(i)

    lane = lax.broadcasted_iota(jnp.int32, (LEV, LANES), 1)

    level = lax.broadcasted_iota(jnp.int32, (LEV, LANES), 0)
    top = lane < 64
    top_before = (lane < 56) | (lane >= 120)

    for field in range(SENT):
        for half in range(2):
            first = jnp.zeros((LEV, LANES), jnp.float32)
            last = first
            for g in range(16):
                row = PAD + (g % 8) + 8 * half + (HALF if g >= 8 else 0)
                value = state[field, row]
                if field == 3:
                    value = jnp.where(level < 4, value, state[4, row])
                turned = shift_lanes(value, 8 * g)
                first = jnp.where((lane >= 8 * g) & (lane < 8 * g + 8), turned, first)
                before = (8 * g - 8) % LANES
                last = jnp.where((lane >= before) & (lane < before + 8), turned, last)
            edge[0, half, field] = first
            edge[1, half, field] = last
    for way, mask in ((0, top), (1, top_before)):
        for pair in range(SENT // 2):
            even, odd = 2 * pair, 2 * pair + 1
            corner[way, 0, pair] = jnp.where(mask, shift_lanes(edge[way, 1, even], 64), edge[way, 1, odd])
            corner[way, 1, pair] = jnp.where(mask, edge[way, 0, even], shift_lanes(edge[way, 0, odd], 64))
    columns = []
    for way, place in ((0, left), (1, right)):
        side = 1 - way
        for number, (a, b, region) in enumerate((
            (edge.at[way], far.at[side], r),
            (corner.at[way, 0], far_corner.at[side, 0], north),
            (corner.at[way, 1], far_corner.at[side, 1], south),
        )):
            copy = pltpu.make_async_remote_copy(
                a, b, col_send.at[way, number], col_recv.at[side, number],
                device_id=(place, region), device_id_type=MESH,
            )
            copy.start()
            columns.append((number, copy))

    main = (state, lap, flux)
    inner(main, ROWS, 10, None)

    in_half = lane % 64
    left_halo, right_halo = in_half < 8, in_half >= 56
    left_group = in_half < 32

    def turn(other):
        code = turns[d] - turns[other]
        code = jnp.where(code < 0, code + 4, code)
        return (
            jnp.where(code == 0, 1.0, jnp.where(code == 2, -1.0, 0.0)),
            jnp.where(code == 1, 1.0, jnp.where(code == 3, -1.0, 0.0)),
        )

    left_turn, right_turn = turn(left), turn(right)
    cosine = jnp.where(left_halo, left_turn[0], jnp.where(right_halo, right_turn[0], 1.0))
    sine = jnp.where(left_halo, left_turn[1], jnp.where(right_halo, right_turn[1], 0.0))
    basis = (cosine, sine)

    def received_sent(block, side, field, mask):
        odd = field % 2 == 1
        if block == 0:
            same, other = far[side, 1, field], far_corner[side, 0, field // 2]
            if odd:
                return shift_lanes(jnp.where(mask, same, other), 64)
            return jnp.where(mask, other, shift_lanes(same, 64))
        if block == 3:
            same, other = far[side, 0, field], far_corner[side, 1, field // 2]
            if odd:
                return jnp.where(mask, shift_lanes(same, 64), other)
            return shift_lanes(jnp.where(mask, other, same), 64)
        return far[side, block - 1, field]

    def received(block, side, field, mask):
        if field < 3:
            return received_sent(block, side, field, mask)
        both = received_sent(block, side, 3, mask)
        return jnp.broadcast_to(both[4 * field - 12:4 * field - 11], (LEV, LANES))

    def build(block):
        def one(field):
            from_left = received(block, 0, field, top_before)
            from_right = received(block, 1, field, top)
            for g in range(8):
                at = 8 * block + g
                low, high = given(field, at), given(field, at + HALF)
                mine = jnp.where(
                    left_group,
                    jnp.where(top, shift_lanes(low, 8), shift_lanes(high, 72)),
                    jnp.where(top, shift_lanes(low, 56), shift_lanes(high, 120)),
                )
                strip[field, at] = jnp.where(
                    left_halo,
                    shift_lanes(from_left, 8 - 8 * g),
                    jnp.where(right_halo, shift_lanes(from_right, 56 - 8 * g), mine),
                )

        for field in range(FIELDS):
            one(field)
        where = pl.ds(8 * block, 8)
        east, north = strip[1, where], strip[2, where]
        strip[1, where] = east * cosine - north * sine
        strip[2, where] = east * sine + north * cosine

    edges = (strip, strip_lap, strip_flux)
    for copy in columns:
        if copy[0] == 0:
            copy[1].wait_recv()
    build(1)
    build(2)
    inner(edges, HALF, 10, basis)

    for copy in rows:
        copy.wait_recv()
    for i in range(PAD):
        spread(i)
        spread(PAD + ROWS + i)
    for copy in columns:
        if copy[0] != 0:
            copy[1].wait_recv()
    build(0)
    build(3)
    outer(((main, ROWS, None), (edges, HALF, basis)))

    h_rows = h_out.reshape(LEV * ROWS, LANES)
    w_rows = w_out.reshape(2 * LEV * ROWS, LANES)
    for i in range(HALF):
        for field in range(3):
            both = strip[field, PAD + i]
            for row, to_left, to_right in ((i, -8, 72), (i + HALF, 56, 8)):
                value = jnp.where(
                    lane < 8,
                    shift_lanes(both, to_left),
                    jnp.where(lane >= 120, shift_lanes(both, to_right), state[field, PAD + row]),
                )
                if field == 0:
                    h_rows[pl.ds(row, LEV, stride=ROWS), :] = value
                else:
                    w_rows[pl.ds((field - 1) * LEV * ROWS + row, LEV, stride=ROWS), :] = value
    for copy in rows + [copy for _, copy in columns]:
        copy.wait_send()


def place(height, wind, out_height, out_wind, sems):
    copies = [
        pltpu.make_async_copy(height, out_height, sems.at[0]),
        pltpu.make_async_copy(wind.at[0], out_wind.at[0], sems.at[1]),
        pltpu.make_async_copy(wind.at[1], out_wind.at[1], sems.at[2]),
    ]
    for copy in copies:
        copy.start()
    for copy in copies:
        copy.wait()


def body(sizes, height, wind, cell_area, pentagon_flags, turn_codes):
    hbm = pl.BlockSpec(memory_space=pltpu.HBM)
    vmem = pl.BlockSpec(memory_space=pltpu.VMEM)
    f32 = jnp.float32
    results = pl.pallas_call(
        functools.partial(kernel, sizes),
        out_shape=(
            jax.ShapeDtypeStruct(height.shape, f32),
            jax.ShapeDtypeStruct(wind.shape, f32),
        ),
        in_specs=[hbm] * 5,
        out_specs=(vmem, vmem),
        scratch_shapes=[
            pltpu.SMEM(turn_codes.shape, jnp.int32),
            pltpu.VMEM((LEV, EXT, LANES), f32),
            pltpu.VMEM((2, LEV, EXT, LANES), f32),
            pltpu.VMEM((EXT, LANES), f32),
            pltpu.VMEM((EXT, LANES), jnp.int32),
            pltpu.VMEM((FIELDS, EXT, LEV, LANES), f32),
            pltpu.VMEM((2, EXT, LEV, LANES), f32),
            pltpu.VMEM((2, EXT, LEV, LANES), f32),
            pltpu.VMEM((FIELDS, STRIP, LEV, LANES), f32),
            pltpu.VMEM((2, STRIP, LEV, LANES), f32),
            pltpu.VMEM((2, STRIP, LEV, LANES), f32),
            pltpu.VMEM((2, 2, SENT, LEV, LANES), f32),
            pltpu.VMEM((2, 2, SENT // 2, LEV, LANES), f32),
            pltpu.VMEM((2, 2, SENT, LEV, LANES), f32),
            pltpu.VMEM((2, 2, SENT // 2, LEV, LANES), f32),
            pltpu.SemaphoreType.DMA((5,)),
            pltpu.SemaphoreType.DMA((2, 4)),
            pltpu.SemaphoreType.DMA((2, 4)),
            pltpu.SemaphoreType.DMA((2, 3)),
            pltpu.SemaphoreType.DMA((2, 3)),
        ],
        compiler_params=pltpu.CompilerParams(
            collective_id=0, has_side_effects=True, vmem_limit_bytes=32 * 1024 * 1024
        ),
    )(*[
        pltpu.with_memory_space_constraint(x, pltpu.HBM)
        for x in (turn_codes, height, wind, cell_area, pentagon_flags)
    ])
    whole = pl.BlockSpec(memory_space=pl.ANY)
    return tuple(pl.pallas_call(
        place,
        out_shape=(
            jax.ShapeDtypeStruct(height.shape, f32),
            jax.ShapeDtypeStruct(wind.shape, f32),
        ),
        in_specs=[whole, whole],
        out_specs=(whole, whole),
        scratch_shapes=[pltpu.SemaphoreType.DMA((3,))],
        compiler_params=pltpu.CompilerParams(vmem_limit_bytes=1024 * 1024),
    )(*results))


def solution(mesh):
    placed = (
        P(None, "region", "diamond"),
        P(None, None, "region", "diamond"),
        P("region", "diamond"),
        P("region", "diamond"),
        P(),
    )
    sizes = (mesh.shape["diamond"], mesh.shape["region"])
    return jax.shard_map(
        functools.partial(body, sizes),
        mesh=mesh,
        in_specs=placed,
        out_specs=(P(None, "region", "diamond"), P(None, None, "region", "diamond")),
        check_vma=False,
    )
```
